32 devices in a mesh: bis: 8 (over z, y), src: 4 (over x, core).
Axes of the slice: x: 2, y: 2, z: 4, core: 2. Of those that a mesh axis runs over, the one named last changes fastest.
Arguments:
- coefficients: float32 [4, 2, 64, 2048], P('src', None, None, 'bis'), may hold values from -6 to 6
- factors: float32 [4, 3, 128, 64, 256], P('src', None, 'bis'), may hold values from -0.375 to 0.375
Outputs:
- potentials: float32 [2, 64, 2048], P(None, 'src', 'bis')
The draws below stay inside these ranges and needn't reach their ends.
All inputs are finite; a program needn't handle non-finite values.
Results may differ from the reference program's by a relative error of at most 0.0001.
Values sent between devices are 32-bit elements; how exact they have to be, the bound alone decides.
No kernel may reach another device: no remote copies, remote signals or barrier semaphores. Data moves between devices by JAX's collectives and lax.ppermute only.
A program may use at most 64 MiB of HBM per device.

```python
import jax
import jax.numpy as jnp
from jax import lax

R = 64
NRHS = 16
LEVELS = 3
B_DEV = 16
S = 4
NB = 128
N_BIS = 8


def steps_of(key, dims, shards, least, largest):
    def one(position, parts):
        heights = jax.random.uniform(jax.random.fold_in(jax.random.fold_in(key, 6), position), (parts,), jnp.float32, least / len(shards), largest / len(shards))
        return jnp.repeat(jnp.exp(heights), dims[position] // parts).reshape((-1,) + (1,) * (len(dims) - position - 1))

    loudness = one(*shards[0])
    for cut in shards[1:]:
        loudness = loudness * one(*cut)
    return loudness


def noise(stream_key, extent, deviation, bound, cuts=(), held_as=jnp.bfloat16):
    level = steps_of(stream_key, extent, cuts, -0.22, 0.18) if cuts else 1.0
    entries = jax.random.normal(stream_key, extent, jnp.float32) * deviation * level
    return jnp.minimum(jnp.maximum(entries, -bound), bound).astype(held_as)


def setup_inputs(seed: int = 0) -> dict:
    keys = jax.random.split(jax.random.key(seed), 3)
    coefficients = noise(keys[0], (S, 2, R, NB * NRHS), 1.0, 6.0, ((0, 4), (3, 8)), jnp.float32)
    factors = noise(keys[1], (S, LEVELS, NB, R, 4 * R), (4 * R) ** -0.5, 0.375, ((0, 4), (2, 8)), jnp.float32)
    return {"coefficients": coefficients, "factors": factors}


def mix_blocks(factor, stacked):
    return jnp.einsum("sboj,sjbk->sobk", factor, stacked, precision=lax.Precision.HIGHEST)


def reference(coefficients, factors):
    groups = coefficients.shape[0]
    state = coefficients.reshape(groups, 2, R, N_BIS * B_DEV, NRHS)
    middle = (N_BIS.bit_length() - 1) // 2
    for level_num in range(LEVELS):
        span = 2 ** (middle + 1 - level_num)
        shaped = state.reshape(groups, 2, R, N_BIS // (2 * span), 2, span * B_DEV, NRHS)
        partner = jnp.flip(shaped, 4).reshape(state.shape)
        stack_re = jnp.concatenate([state[:, 0], -state[:, 1], partner[:, 0], -partner[:, 1]], axis=1)
        stack_im = jnp.concatenate([state[:, 1], state[:, 0], partner[:, 1], partner[:, 0]], axis=1)
        factor = factors[:, level_num]
        state = jnp.stack([mix_blocks(factor, stack_re), mix_blocks(factor, stack_im)], axis=1)
    total = jnp.sum(state, axis=0)
    return total.reshape(2, R, N_BIS * B_DEV * NRHS)
```

```python
import functools
import jax
import jax.numpy as jnp
from jax import lax
from jax.experimental import pallas as pl
from jax.experimental.pallas import tpu as pltpu
from jax.sharding import PartitionSpec as P

LEVELS = 3
VMEM = pltpu.MemorySpace.VMEM


def swapped(value, axis, mask):
    pairs = [(source, source ^ mask) for source in range(lax.axis_size(axis))]
    return lax.ppermute(value, axis, pairs)


def split(value):
    high = value.astype(jnp.bfloat16)
    low = (value - high.astype(jnp.float32)).astype(jnp.bfloat16)
    return high, low


def prepare_kernel(f_ref, high_ref, low_ref):
    lane = lax.broadcasted_iota(jnp.int32, (64, 256), 1)
    sign = jnp.where((lane // 64) % 2 == 0, 1.0, -1.0).astype(jnp.float32)

    def one(i, carry):
        f = f_ref[i]
        swap = jnp.concatenate(
            [pltpu.roll(f[:, :128], 64, 1), pltpu.roll(f[:, 128:], 64, 1)], axis=1
        )
        full = jnp.concatenate([f * sign, swap], axis=0)
        high, low = split(full)
        high_ref[i] = high
        low_ref[i] = low
        return carry

    lax.fori_loop(0, f_ref.shape[0], one, 0, unroll=2)


def product(own, partner, high_ref, low_ref, blocks, width):
    high, low = split(jnp.concatenate([own, partner], axis=1))
    outs = []
    dims = (((1,), (1,)), ((), ()))
    for b in range(blocks):
        rows = slice(b * width, (b + 1) * width)
        both = jnp.concatenate([high[rows], low[rows]], axis=0)
        first = lax.dot_general(both, high_ref[b], dims, preferred_element_type=jnp.float32)
        second = lax.dot_general(high[rows], low_ref[b], dims, preferred_element_type=jnp.float32)
        outs.append(first[:width] + first[width:] + second)
    return jnp.concatenate(outs, axis=0)


def first_kernel(own_ref, partner_ref, high_ref, low_ref, out_ref, *, blocks, width):
    own = own_ref[...].T
    partner = partner_ref[...].T
    out_ref[...] = product(own, partner, high_ref, low_ref, blocks, width)


def middle_kernel(own_ref, partner_ref, high_ref, low_ref, out_ref, *, blocks, width):
    out_ref[...] = product(own_ref[...], partner_ref[...], high_ref, low_ref, blocks, width)


def last_kernel(own_ref, partner_ref, high_ref, low_ref, out_ref, *, blocks, width):
    out_ref[...] = product(own_ref[...], partner_ref[...], high_ref, low_ref, blocks, width).T


def call(kernel, outs, *args):
    return pl.pallas_call(
        kernel,
        out_shape=outs,
        in_specs=[pl.BlockSpec(memory_space=VMEM)] * len(args),
        out_specs=jax.tree.map(lambda _: pl.BlockSpec(memory_space=VMEM), outs),
        compiler_params=pltpu.CompilerParams(vmem_limit_bytes=32 * 2**20),
    )(*args)


def per_device(coefficients, factors):
    middle = (lax.axis_size("bis").bit_length() - 1) // 2
    rank, columns, blocks = coefficients.shape[2], coefficients.shape[3], factors.shape[2]
    kw = dict(blocks=blocks, width=columns // blocks)
    raw = coefficients.reshape(2 * rank, columns)
    got = swapped(raw, "bis", 2 ** (middle + 1))
    weights = []
    for level in range(LEVELS):
        shape = jax.ShapeDtypeStruct((blocks, 2 * rank, 4 * rank), jnp.bfloat16)
        weights.append(call(prepare_kernel, [shape, shape], factors[0, level]))
    st = jax.ShapeDtypeStruct((columns, 2 * rank), jnp.float32)
    state = call(functools.partial(first_kernel, **kw), st, raw, got, *weights[0])
    got = swapped(state, "bis", 2 ** middle)
    state = call(functools.partial(middle_kernel, **kw), st, state, got, *weights[1])
    got = swapped(state, "bis", 2 ** (middle - 1))
    st = jax.ShapeDtypeStruct((2 * rank, columns), jnp.float32)
    total = call(functools.partial(last_kernel, **kw), st, state, got, *weights[2])
    groups = lax.axis_size("src")
    me = lax.axis_index("src")
    parts = total.reshape(2, groups, rank // groups, columns)
    mine = lax.dynamic_index_in_dim(parts, me, 1, keepdims=False)
    others = [
        swapped(lax.dynamic_index_in_dim(parts, me ^ m, 1, keepdims=False), "src", m)
        for m in range(1, groups)
    ]
    for o in others:
        mine = mine + o
    return mine


def solution(mesh):
    placed = (P("src", None, None, "bis"), P("src", None, "bis", None, None))
    return jax.shard_map(
        per_device, mesh=mesh, in_specs=placed, out_specs=P(None, "src", "bis"), check_vma=False
    )
```

```python
import functools
import jax
import jax.numpy as jnp
from jax import lax
from jax.experimental import pallas as pl
from jax.experimental.pallas import tpu as pltpu
from jax.sharding import PartitionSpec as P

LEVELS = 3
CHUNKS = 2
VMEM = pl.BlockSpec(memory_space=pltpu.MemorySpace.VMEM)
SMEM = pl.BlockSpec(memory_space=pltpu.MemorySpace.SMEM)
HBM = pl.BlockSpec(memory_space=pltpu.MemorySpace.HBM)


def swapped(value, axis, mask):
    pairs = [(source, source ^ mask) for source in range(lax.axis_size(axis))]
    return lax.ppermute(value, axis, pairs)


def split(value):
    high = value.astype(jnp.bfloat16)
    low = (value - high.astype(jnp.float32)).astype(jnp.bfloat16)
    return high, low


def advance(own, partner, fh, fl, width):
    blocks, rank, depth = fh.shape
    n = own.shape[1]
    fh, fl = fh.reshape(blocks * rank, depth), fl.reshape(blocks * rank, depth)
    re, im, other_re, other_im = own[:rank], own[rank:], partner[:rank], partner[rank:]
    stack = jnp.concatenate(
        [
            jnp.concatenate([re, -im, other_re, -other_im], axis=0),
            jnp.concatenate([im, re, other_im, other_re], axis=0),
        ],
        axis=1,
    )
    xh, xl = split(stack)
    dot = functools.partial(jnp.dot, preferred_element_type=jnp.float32)
    full = dot(fh, xh) + dot(fh, xl) + dot(fl, xh)
    block = lax.broadcasted_iota(jnp.int32, (rank, n), 1) // width
    halves = []
    for q in range(2):
        out = full[:rank, q * n : (q + 1) * n]
        for b in range(1, blocks):
            out = jnp.where(block == b, full[b * rank : (b + 1) * rank, q * n : (q + 1) * n], out)
        halves.append(out)
    return jnp.concatenate(halves, axis=0)


def arrange_kernel(x_hbm, *refs):
    *outs, sems = refs
    n = outs[0].shape[1]
    copies = [
        pltpu.make_async_copy(x_hbm.at[:, i * n : (i + 1) * n], o, sems.at[i])
        for i, o in enumerate(outs)
    ]
    for c in copies:
        c.start()
    for c in copies:
        c.wait()


def prepare_kernel(f_hbm, *refs):
    *outs, f_ref, sems = refs
    copies = [
        pltpu.make_async_copy(f_hbm.at[0, i], f_ref.at[i], sems.at[i]) for i in range(LEVELS)
    ]
    for c in copies:
        c.start()
    for level in range(LEVELS):
        copies[level].wait()
        high_ref, low_ref = outs[2 * level : 2 * level + 2]

        def one(b, carry):
            high_ref[b], low_ref[b] = split(f_ref[level, b])
            return carry

        lax.fori_loop(0, f_ref.shape[1], one, 0, unroll=4)


def middle_kernel(own_ref, got_ref, fh_ref, fl_ref, out_ref, *, i, width):
    blocks = own_ref.shape[1] // width
    rows = slice(i * blocks, (i + 1) * blocks)
    out_ref[...] = advance(own_ref[...], got_ref[...], fh_ref[rows], fl_ref[rows], width)


def turn_kernel(me_ref, done_ref, own_ref, got_ref, fh_ref, fl_ref, *out_refs, i, width):
    blocks = own_ref.shape[1] // width
    rows = slice(i * blocks, (i + 1) * blocks)
    total = advance(own_ref[...], got_ref[...], fh_ref[rows], fl_ref[rows], width)
    total = jnp.concatenate([total, done_ref[...]] if i == 0 else [done_ref[...], total], axis=1)
    groups = len(out_refs)
    share = total.shape[0] // 2 // groups
    for g in range(groups):
        part = jnp.stack([total[q * share : (q + 1) * share] for q in (g, groups + g)])
        m = me_ref[0] ^ g
        for j in range(groups):

            @pl.when(m == j)
            def _():
                out_refs[j][...] = part


def sum_kernel(*refs):
    *parts, out_ref = refs
    total = parts[0][...]
    for r in parts[1:]:
        total = total + r[...]
    out_ref[...] = total


def call(kernel, outs, *args, specs=None, limit=16, scratch=(), name=None):
    return pl.pallas_call(
        kernel,
        out_shape=outs,
        in_specs=specs or [VMEM] * len(args),
        out_specs=jax.tree.map(lambda _: VMEM, outs),
        scratch_shapes=scratch,
        compiler_params=pltpu.CompilerParams(vmem_limit_bytes=limit * 2**20),
        name=name,
    )(*args)


def per_device(coefficients, factors):
    middle = (lax.axis_size("bis").bit_length() - 1) // 2
    rank, columns, blocks = coefficients.shape[2], coefficients.shape[3], factors.shape[2]
    width = columns // blocks
    groups = lax.axis_size("src")
    f32 = jnp.float32
    raw = coefficients.reshape(2 * rank, columns)
    part = jax.ShapeDtypeStruct((2 * rank, columns // CHUNKS), f32)
    step = columns // CHUNKS
    states = [raw[:, i * step : (i + 1) * step] for i in range(CHUNKS)]
    me = jnp.reshape(lax.axis_index("src"), (1,)).astype(jnp.int32)
    piece = jax.ShapeDtypeStruct((2, rank // groups, columns), f32)
    gots = [swapped(s, "bis", 2 ** (middle + 1)) for s in states]
    half = jax.ShapeDtypeStruct(factors.shape[2:], jnp.bfloat16)
    halves = call(
        prepare_kernel, [half] * (2 * LEVELS), factors, specs=[HBM],
        scratch=[pltpu.VMEM(factors.shape[1:], f32), pltpu.SemaphoreType.DMA((LEVELS,))],
        name="prepare",
    )
    order = tuple(reversed(range(CHUNKS)))
    for level in range(LEVELS):
        for i in order:
            kw = dict(i=i, width=width)
            if (level, i) != (LEVELS - 1, order[-1]):
                states[i] = call(
                    functools.partial(middle_kernel, **kw), part, states[i], gots[i],
                    *halves[2 * level : 2 * level + 2], name=f"level{level}_{i}",
                )
            else:
                pieces = call(
                    functools.partial(turn_kernel, **kw), [piece] * groups,
                    me, states[order[0]], states[i], gots[i], *halves[2 * level : 2 * level + 2],
                    specs=[SMEM] + [VMEM] * 5, name=f"level{level}_{i}",
                )
            if level < LEVELS - 1:
                gots[i] = swapped(states[i], "bis", 2 ** (middle - level))
    parts = [pieces[0]] + [swapped(pieces[m], "src", m) for m in reversed(range(1, groups))]
    return call(sum_kernel, piece, *parts, name="total")


def solution(mesh):
    placed = (P("src", None, None, "bis"), P("src", None, "bis", None, None))
    return jax.shard_map(
        per_device, mesh=mesh, in_specs=placed, out_specs=P(None, "src", "bis"), check_vma=False
    )
```

```python
import functools
import jax
import jax.numpy as jnp
from jax import lax
from jax.experimental import pallas as pl
from jax.experimental.pallas import tpu as pltpu
from jax.sharding import PartitionSpec as P

LEVELS = 3
CHUNKS = 2
VMEM = pl.BlockSpec(memory_space=pltpu.MemorySpace.VMEM)
SMEM = pl.BlockSpec(memory_space=pltpu.MemorySpace.SMEM)
ANY = pl.BlockSpec(memory_space=pl.ANY)


def swapped(value, axis, mask):
    pairs = [(source, source ^ mask) for source in range(lax.axis_size(axis))]
    return lax.ppermute(value, axis, pairs)


def split(value):
    high = value.astype(jnp.bfloat16)
    low = (value - high.astype(jnp.float32)).astype(jnp.bfloat16)
    return high, low


def product(state, factor, width):
    rank, n = state.shape[0] // 2, state.shape[1]
    re, im = state[:rank], state[rank:]
    stack = jnp.concatenate(
        [jnp.concatenate([re, -im], axis=0), jnp.concatenate([im, re], axis=0)], axis=1
    )
    lane = lax.broadcasted_iota(jnp.int32, stack.shape, 1) % n
    zero = jnp.zeros_like(stack)
    stack = jnp.concatenate(
        [jnp.where(lane < n // 2, stack, zero), jnp.where(lane < n // 2, zero, stack)], axis=0
    )
    high, low = split(stack)
    rows = factor.shape[0] // 2
    dot = functools.partial(jnp.dot, preferred_element_type=jnp.float32)
    full = dot(factor[:rows], high) + dot(factor[:rows], low) + dot(factor[rows:], high)
    block = lax.broadcasted_iota(jnp.int32, (rank, 2 * n), 1) % (n // 2) // width
    out = full[:rank]
    for p in range(1, rows // rank):
        out = jnp.where(block == p, full[p * rank : (p + 1) * rank], out)
    return jnp.concatenate([out[:, :n], out[:, n:]], axis=0)


def prepare_kernel(f_hbm, *refs):
    *outs, f_ref, sems = refs
    copies = [
        pltpu.make_async_copy(f_hbm.at[0, i], f_ref.at[i], sems.at[i]) for i in range(LEVELS)
    ]
    for c in copies:
        c.start()
    rank, depth = f_ref.shape[2:]
    half = depth // 2
    for level in range(LEVELS):
        copies[level].wait()
        chunks, rows, _ = outs[2 * level].shape
        rows = rows // 2
        per = rows // rank
        for c in range(chunks):
            for u in range(2):
                first = (2 * c + u) * per
                high, low = split(f_ref[level, first : first + per].reshape(rows, depth))
                side = slice(u * half, (u + 1) * half)
                for part in range(2):
                    out = outs[2 * level + part]
                    out[c, :rows, side] = high[:, part * half : (part + 1) * half]
                    out[c, rows:, side] = low[:, part * half : (part + 1) * half]


def own_kernel(own_ref, f_ref, out_ref, *, i, width):
    out_ref[...] = product(own_ref[...], f_ref[i], width)


def level_kernel(base_ref, got_ref, f_ref, out_ref, *, i, width):
    out_ref[...] = base_ref[...] + product(got_ref[...], f_ref[i], width)


def last_kernel(me_ref, done_ref, base_ref, got_ref, f_ref, *refs, i, width):
    *outs, total_ref = refs
    n = got_ref.shape[1]
    other = 1 - i
    total_ref[:, other * n : (other + 1) * n] = done_ref[...]
    total_ref[:, i * n : (i + 1) * n] = base_ref[...] + product(got_ref[...], f_ref[i], width)
    rank = total_ref.shape[0] // 2
    share = rank // len(outs)
    for m, out in enumerate(outs):
        start = pl.multiple_of((me_ref[0] ^ m) * share, share)
        for q in range(2):
            out[q] = total_ref[pl.ds(q * rank + start, share), :]


def sum_kernel(*refs):
    *parts, out_ref = refs
    total = parts[0][...]
    for r in parts[1:]:
        total = total + r[...]
    out_ref[...] = total


def call(kernel, outs, *args, specs=None, scratch=(), name=None):
    return pl.pallas_call(
        kernel,
        out_shape=outs,
        in_specs=specs or [VMEM] * len(args),
        out_specs=jax.tree.map(lambda _: VMEM, outs),
        scratch_shapes=scratch,
        compiler_params=pltpu.CompilerParams(vmem_limit_bytes=16 * 2**20),
        name=name,
    )(*args)


def per_device(coefficients, factors):
    middle = (lax.axis_size("bis").bit_length() - 1) // 2
    rank, columns, blocks = coefficients.shape[2], coefficients.shape[3], factors.shape[2]
    width = columns // blocks
    step = columns // CHUNKS
    groups = lax.axis_size("src")
    f32 = jnp.float32
    raw = coefficients.reshape(2 * rank, columns)
    states = [raw[:, i * step : (i + 1) * step] for i in range(CHUNKS)]
    gots = [swapped(s, "bis", 2 ** (middle + 1)) for s in states]
    stacked = jax.ShapeDtypeStruct((CHUNKS, blocks // CHUNKS * rank, 4 * rank), jnp.bfloat16)
    halves = call(
        prepare_kernel, [stacked] * (2 * LEVELS), factors, specs=[ANY],
        scratch=[pltpu.VMEM(factors.shape[1:], f32), pltpu.SemaphoreType.DMA((LEVELS,))],
        name="prepare",
    )
    me = jnp.reshape(lax.axis_index("src"), (1,)).astype(jnp.int32)
    shape = jax.ShapeDtypeStruct((2 * rank, step), f32)
    piece = jax.ShapeDtypeStruct((2, rank // groups, columns), f32)
    order = tuple(reversed(range(CHUNKS)))
    for level in range(LEVELS):
        own, other = halves[2 * level : 2 * level + 2]
        for i in order:
            kw = dict(i=i, width=width)
            base = call(
                functools.partial(own_kernel, **kw), shape, states[i], own, name=f"own{level}_{i}"
            )
            if (level, i) == (LEVELS - 1, order[-1]):
                pieces = call(
                    functools.partial(last_kernel, **kw), [piece] * groups,
                    me, states[order[0]], base, gots[i], other, specs=[SMEM] + [VMEM] * 4,
                    scratch=[pltpu.VMEM((2 * rank, columns), f32)], name="last",
                )
                continue
            states[i] = call(
                functools.partial(level_kernel, **kw), shape, base, gots[i], other,
                name=f"level{level}_{i}",
            )
            if level < LEVELS - 1:
                gots[i] = swapped(states[i], "bis", 2 ** (middle - level))
    parts = [pieces[0]] + [swapped(pieces[m], "src", m) for m in reversed(range(1, groups))]
    return call(sum_kernel, piece, *parts, name="total")


def solution(mesh):
    placed = (P("src", None, None, "bis"), P("src", None, "bis", None, None))
    return jax.shard_map(
        per_device, mesh=mesh, in_specs=placed, out_specs=P(None, "src", "bis"), check_vma=False
    )
```

```python
import functools
import jax
import jax.numpy as jnp
from jax import lax
from jax.experimental import pallas as pl
from jax.experimental.pallas import tpu as pltpu
from jax.sharding import PartitionSpec as P

LEVELS = 3
CHUNKS = 2
VMEM = pl.BlockSpec(memory_space=pltpu.MemorySpace.VMEM)
SMEM = pl.BlockSpec(memory_space=pltpu.MemorySpace.SMEM)
ANY = pl.BlockSpec(memory_space=pl.ANY)


def swapped(value, axis, mask):
    pairs = [(source, source ^ mask) for source in range(lax.axis_size(axis))]
    return lax.ppermute(value, axis, pairs)


def split(value):
    high = value.astype(jnp.bfloat16)
    low = (value - high.astype(jnp.float32)).astype(jnp.bfloat16)
    return high, low


def product(state, factor, width):
    rank, n = state.shape[0] // 2, state.shape[1]
    re, im = state[:rank], state[rank:]
    stack = jnp.concatenate(
        [jnp.concatenate([re, -im], axis=0), jnp.concatenate([im, re], axis=0)], axis=1
    )
    lane = lax.broadcasted_iota(jnp.int32, stack.shape, 1) % n
    zero = jnp.zeros_like(stack)
    stack = jnp.concatenate(
        [jnp.where(lane < n // 2, stack, zero), jnp.where(lane < n // 2, zero, stack)], axis=0
    )
    high, low = split(stack)
    rows = factor.shape[0] // 2
    dot = functools.partial(jnp.dot, preferred_element_type=jnp.float32)
    full = dot(factor[:rows], high) + dot(factor[:rows], low) + dot(factor[rows:], high)
    block = lax.broadcasted_iota(jnp.int32, (rank, 2 * n), 1) % (n // 2) // width
    out = full[:rank]
    for p in range(1, rows // rank):
        out = jnp.where(block == p, full[p * rank : (p + 1) * rank], out)
    return jnp.concatenate([out[:, :n], out[:, n:]], axis=0)


def arrange_kernel(me_ref, first_ref, second_ref, *outs):
    first, second = first_ref[...], second_ref[...]
    swap = me_ref[0] % 2 == 1
    re, im = jnp.where(swap, second, first), jnp.where(swap, first, second)
    n = outs[0].shape[1]
    for i, out in enumerate(outs):
        cols = slice(i * n, (i + 1) * n)
        out[...] = jnp.concatenate([re[:, cols], im[:, cols]], axis=0)


def prepare_kernel(f_hbm, *refs):
    *outs, f_ref, sems = refs
    copies = [
        pltpu.make_async_copy(f_hbm.at[0, i], f_ref.at[i], sems.at[i]) for i in range(LEVELS)
    ]
    for c in copies:
        c.start()
    rank, depth = f_ref.shape[2:]
    half = depth // 2
    for level in range(LEVELS):
        copies[level].wait()
        chunks, rows, _ = outs[2 * level].shape
        rows = rows // 2
        per = rows // rank
        for c in range(chunks):
            for u in range(2):
                first = (2 * c + u) * per
                high, low = split(f_ref[level, first : first + per].reshape(rows, depth))
                side = slice(u * half, (u + 1) * half)
                for part in range(2):
                    out = outs[2 * level + part]
                    out[c, :rows, side] = high[:, part * half : (part + 1) * half]
                    out[c, rows:, side] = low[:, part * half : (part + 1) * half]


def own_kernel(own_ref, f_ref, out_ref, *, i, width):
    out_ref[...] = product(own_ref[...], f_ref[i], width)


def level_kernel(base_ref, got_ref, f_ref, out_ref, *, i, width):
    out_ref[...] = base_ref[...] + product(got_ref[...], f_ref[i], width)


def last_kernel(me_ref, done_ref, base_ref, got_ref, f_ref, *refs, i, width):
    *outs, total_ref = refs
    n = got_ref.shape[1]
    other = 1 - i
    total_ref[:, other * n : (other + 1) * n] = done_ref[...]
    total_ref[:, i * n : (i + 1) * n] = base_ref[...] + product(got_ref[...], f_ref[i], width)
    rank = total_ref.shape[0] // 2
    share = rank // len(outs)
    for m, out in enumerate(outs):
        start = pl.multiple_of((me_ref[0] ^ m) * share, share)
        for q in range(2):
            out[q] = total_ref[pl.ds(q * rank + start, share), :]


def sum_kernel(*refs):
    *parts, out_ref = refs
    total = parts[0][...]
    for r in parts[1:]:
        total = total + r[...]
    out_ref[...] = total


def call(kernel, outs, *args, specs=None, scratch=(), name=None):
    return pl.pallas_call(
        kernel,
        out_shape=outs,
        in_specs=specs or [VMEM] * len(args),
        out_specs=jax.tree.map(lambda _: VMEM, outs),
        scratch_shapes=scratch,
        compiler_params=pltpu.CompilerParams(vmem_limit_bytes=16 * 2**20),
        name=name,
    )(*args)


def per_device(coefficients, factors):
    middle = (lax.axis_size("bis").bit_length() - 1) // 2
    rank, columns, blocks = coefficients.shape[2], coefficients.shape[3], factors.shape[2]
    width = columns // blocks
    step = columns // CHUNKS
    groups = lax.axis_size("src")
    f32 = jnp.float32
    me = lax.axis_index("src")
    where = jnp.reshape(me, (1,)).astype(jnp.int32)
    shape = jax.ShapeDtypeStruct((2 * rank, step), f32)
    first = lax.dynamic_index_in_dim(coefficients[0], me % 2, 0, keepdims=False)
    first, rest = lax.optimization_barrier((first, 1 - me % 2))
    second = lax.dynamic_index_in_dim(coefficients[0], rest, 0, keepdims=False)
    states = list(
        call(
            arrange_kernel, [shape] * CHUNKS, where, first, second, specs=[SMEM] + [VMEM] * 2,
            name="arrange",
        )
    )
    gots = [swapped(s, "bis", 2 ** (middle + 1)) for s in states]
    stacked = jax.ShapeDtypeStruct((CHUNKS, blocks // CHUNKS * rank, 4 * rank), jnp.bfloat16)
    halves = call(
        prepare_kernel, [stacked] * (2 * LEVELS), factors, specs=[ANY],
        scratch=[pltpu.VMEM(factors.shape[1:], f32), pltpu.SemaphoreType.DMA((LEVELS,))],
        name="prepare",
    )
    piece = jax.ShapeDtypeStruct((2, rank // groups, columns), f32)
    order = tuple(reversed(range(CHUNKS)))
    for level in range(LEVELS):
        own, other = halves[2 * level : 2 * level + 2]
        for i in order:
            kw = dict(i=i, width=width)
            base = call(
                functools.partial(own_kernel, **kw), shape, states[i], own, name=f"own{level}_{i}"
            )
            if (level, i) == (LEVELS - 1, order[-1]):
                pieces = call(
                    functools.partial(last_kernel, **kw), [piece] * groups,
                    where, states[order[0]], base, gots[i], other, specs=[SMEM] + [VMEM] * 4,
                    scratch=[pltpu.VMEM((2 * rank, columns), f32)], name="last",
                )
                continue
            states[i] = call(
                functools.partial(level_kernel, **kw), shape, base, gots[i], other,
                name=f"level{level}_{i}",
            )
            if level < LEVELS - 1:
                gots[i] = swapped(states[i], "bis", 2 ** (middle - level))
    parts = [pieces[0]] + [swapped(pieces[m], "src", m) for m in reversed(range(1, groups))]
    return call(sum_kernel, piece, *parts, name="total")


def solution(mesh):
    placed = (P("src", None, None, "bis"), P("src", None, "bis", None, None))
    return jax.shard_map(
        per_device, mesh=mesh, in_specs=placed, out_specs=P(None, "src", "bis"), check_vma=False
    )
```

```python
import functools
import jax
import jax.numpy as jnp
from jax import lax
from jax.experimental import pallas as pl
from jax.experimental.pallas import tpu as pltpu
from jax.sharding import PartitionSpec as P

LEVELS = 3
CHUNKS = 2
VMEM = pl.BlockSpec(memory_space=pltpu.MemorySpace.VMEM)
SMEM = pl.BlockSpec(memory_space=pltpu.MemorySpace.SMEM)
ANY = pl.BlockSpec(memory_space=pl.ANY)


def swapped(value, axis, mask):
    pairs = [(source, source ^ mask) for source in range(lax.axis_size(axis))]
    return lax.ppermute(value, axis, pairs)


def split(value):
    high = value.astype(jnp.bfloat16)
    low = (value - high.astype(jnp.float32)).astype(jnp.bfloat16)
    return high, low


def product(state, factor, width):
    rank, n = state.shape[0] // 2, state.shape[1]
    re, im = state[:rank], state[rank:]
    stack = jnp.concatenate(
        [jnp.concatenate([re, -im], axis=0), jnp.concatenate([im, re], axis=0)], axis=1
    )
    lane = lax.broadcasted_iota(jnp.int32, stack.shape, 1) % n
    zero = jnp.zeros_like(stack)
    stack = jnp.concatenate(
        [jnp.where(lane < n // 2, stack, zero), jnp.where(lane < n // 2, zero, stack)], axis=0
    )
    high, low = split(stack)
    rows = factor.shape[0] // 2
    dot = functools.partial(jnp.dot, preferred_element_type=jnp.float32)
    full = dot(factor[:rows], high) + dot(factor[:rows], low) + dot(factor[rows:], high)
    block = lax.broadcasted_iota(jnp.int32, (rank, 2 * n), 1) % (n // 2) // width
    out = full[:rank]
    for p in range(1, rows // rank):
        out = jnp.where(block == p, full[p * rank : (p + 1) * rank], out)
    return jnp.concatenate([out[:, :n], out[:, n:]], axis=0)


def prepare_kernel(f_hbm, *refs):
    outs, f_ref = refs, f_hbm.at[0]
    rank, depth = f_ref.shape[2:]
    half = depth // 2
    for level in range(LEVELS):
        chunks, rows, _ = outs[2 * level].shape
        rows = rows // 2
        per = rows // rank
        for c in range(chunks):
            for u in range(2):
                first = (2 * c + u) * per
                high, low = split(f_ref[level, first : first + per].reshape(rows, depth))
                side = slice(u * half, (u + 1) * half)
                for part in range(2):
                    out = outs[2 * level + part]
                    out[c, :rows, side] = high[:, part * half : (part + 1) * half]
                    out[c, rows:, side] = low[:, part * half : (part + 1) * half]


def own_kernel(own_ref, f_ref, out_ref, *, i, width):
    out_ref[...] = product(own_ref[...], f_ref[i], width)


def owns_kernel(*refs, width):
    f_ref = refs[CHUNKS]
    for i, out in enumerate(refs[CHUNKS + 1 :]):
        out[...] = product(refs[i][...], f_ref[i], width)


def level_kernel(base_ref, got_ref, f_ref, out_ref, *, i, width):
    out_ref[...] = base_ref[...] + product(got_ref[...], f_ref[i], width)


def last_kernel(me_ref, done_ref, base_ref, got_ref, f_ref, *refs, i, width):
    *outs, total_ref = refs
    n = got_ref.shape[1]
    other = 1 - i
    total_ref[:, other * n : (other + 1) * n] = done_ref[...]
    total_ref[:, i * n : (i + 1) * n] = base_ref[...] + product(got_ref[...], f_ref[i], width)
    rank = total_ref.shape[0] // 2
    share = rank // len(outs)
    for m, out in enumerate(outs):
        start = pl.multiple_of((me_ref[0] ^ m) * share, share)
        for q in range(2):
            out[q] = total_ref[pl.ds(q * rank + start, share), :]


def sum_kernel(*refs):
    *parts, out_ref = refs
    total = parts[0][...]
    for r in parts[1:]:
        total = total + r[...]
    out_ref[...] = total


def call(kernel, outs, *args, specs=None, scratch=(), name=None):
    return pl.pallas_call(
        kernel,
        out_shape=outs,
        in_specs=specs or [VMEM] * len(args),
        out_specs=jax.tree.map(lambda _: VMEM, outs),
        scratch_shapes=scratch,
        compiler_params=pltpu.CompilerParams(vmem_limit_bytes=16 * 2**20),
        name=name,
    )(*args)


def per_device(coefficients, factors):
    middle = (lax.axis_size("bis").bit_length() - 1) // 2
    rank, columns, blocks = coefficients.shape[2], coefficients.shape[3], factors.shape[2]
    width = columns // blocks
    step = columns // CHUNKS
    groups = lax.axis_size("src")
    f32 = jnp.float32
    raw = coefficients.reshape(2 * rank, columns)
    one = raw[:, step:]
    one, rest = lax.optimization_barrier((one, raw))
    states = [rest[:, :step], one]
    gots = [swapped(s, "bis", 2 ** (middle + 1)) for s in states]
    stacked = jax.ShapeDtypeStruct((CHUNKS, blocks // CHUNKS * rank, 4 * rank), jnp.bfloat16)
    halves = call(
        prepare_kernel, [stacked] * (2 * LEVELS), factors, name="prepare",
    )
    me = jnp.reshape(lax.axis_index("src"), (1,)).astype(jnp.int32)
    shape = jax.ShapeDtypeStruct((2 * rank, step), f32)
    piece = jax.ShapeDtypeStruct((2, rank // groups, columns), f32)
    order = tuple(reversed(range(CHUNKS)))
    for level in range(LEVELS):
        own, other = halves[2 * level : 2 * level + 2]
        for i in order:
            kw = dict(i=i, width=width)
            if level:
                base = call(
                    functools.partial(own_kernel, **kw), shape, states[i], own, name=f"own{level}_{i}"
                )
            else:
                if i == order[0]:
                    bases = call(
                        functools.partial(owns_kernel, width=width), [shape] * CHUNKS, *states, own,
                        name="own0",
                    )
                base = bases[i]
            if (level, i) == (LEVELS - 1, order[-1]):
                pieces = call(
                    functools.partial(last_kernel, **kw), [piece] * groups,
                    me, states[order[0]], base, gots[i], other, specs=[SMEM] + [VMEM] * 4,
                    scratch=[pltpu.VMEM((2 * rank, columns), f32)], name="last",
                )
                continue
            states[i] = call(
                functools.partial(level_kernel, **kw), shape, base, gots[i], other,
                name=f"level{level}_{i}",
            )
            if level < LEVELS - 1:
                gots[i] = swapped(states[i], "bis", 2 ** (middle - level))
    parts = [pieces[0]] + [swapped(pieces[m], "src", m) for m in reversed(range(1, groups))]
    return call(sum_kernel, piece, *parts, name="total")


def solution(mesh):
    placed = (P("src", None, None, "bis"), P("src", None, "bis", None, None))
    return jax.shard_map(
        per_device, mesh=mesh, in_specs=placed, out_specs=P(None, "src", "bis"), check_vma=False
    )
```

```python
import functools
import jax
import jax.numpy as jnp
from jax import lax
from jax.experimental import pallas as pl
from jax.experimental.pallas import tpu as pltpu
from jax.sharding import PartitionSpec as P

LEVELS = 3
CHUNKS = 2
VMEM = pl.BlockSpec(memory_space=pltpu.MemorySpace.VMEM)
SMEM = pl.BlockSpec(memory_space=pltpu.MemorySpace.SMEM)
ANY = pl.BlockSpec(memory_space=pl.ANY)


def swapped(value, axis, mask):
    pairs = [(source, source ^ mask) for source in range(lax.axis_size(axis))]
    return lax.ppermute(value, axis, pairs)


def split(value):
    high = value.astype(jnp.bfloat16)
    low = (value - high.astype(jnp.float32)).astype(jnp.bfloat16)
    return high, low


def product(state, factor, width):
    rank, n = state.shape[0] // 2, state.shape[1]
    re, im = state[:rank], state[rank:]
    stack = jnp.concatenate(
        [jnp.concatenate([re, -im], axis=0), jnp.concatenate([im, re], axis=0)], axis=1
    )
    lane = lax.broadcasted_iota(jnp.int32, stack.shape, 1) % n
    zero = jnp.zeros_like(stack)
    stack = jnp.concatenate(
        [jnp.where(lane < n // 2, stack, zero), jnp.where(lane < n // 2, zero, stack)], axis=0
    )
    high, low = split(stack)
    rows = factor.shape[0] // 2
    dot = functools.partial(jnp.dot, preferred_element_type=jnp.float32)
    full = dot(factor[:rows], high) + dot(factor[:rows], low) + dot(factor[rows:], high)
    block = lax.broadcasted_iota(jnp.int32, (rank, 2 * n), 1) % (n // 2) // width
    out = full[:rank]
    for p in range(1, rows // rank):
        out = jnp.where(block == p, full[p * rank : (p + 1) * rank], out)
    return jnp.concatenate([out[:, :n], out[:, n:]], axis=0)


def prepare_kernel(f_hbm, *refs):
    outs, f_ref = refs, f_hbm.at[0]
    rank, depth = f_ref.shape[2:]
    half = depth // 2
    for level in range(LEVELS):
        chunks, rows, _ = outs[2 * level].shape
        rows = rows // 2
        per = rows // rank
        for c in range(chunks):
            for u in range(2):
                first = (2 * c + u) * per
                high, low = split(f_ref[level, first : first + per].reshape(rows, depth))
                side = slice(u * half, (u + 1) * half)
                for part in range(2):
                    out = outs[2 * level + part]
                    out[c, :rows, side] = high[:, part * half : (part + 1) * half]
                    out[c, rows:, side] = low[:, part * half : (part + 1) * half]


def own_kernel(own_ref, f_ref, out_ref, *, i, width):
    out_ref[...] = product(own_ref[...], f_ref[i], width)


def owns_kernel(*refs, width):
    f_ref = refs[CHUNKS]
    for i, out in enumerate(refs[CHUNKS + 1 :]):
        out[...] = product(refs[i][...], f_ref[i], width)


def level_kernel(base_ref, got_ref, f_ref, out_ref, *, i, width):
    out_ref[...] = base_ref[...] + product(got_ref[...], f_ref[i], width)


def both_kernel(own_ref, got_ref, f_ref, g_ref, out_ref, *, i, width):
    out_ref[...] = product(own_ref[...], f_ref[i], width) + product(got_ref[...], g_ref[i], width)


def last_kernel(me_ref, done_ref, base_ref, got_ref, f_ref, *refs, i, width):
    *outs, total_ref = refs
    n = got_ref.shape[1]
    other = 1 - i
    total_ref[:, other * n : (other + 1) * n] = done_ref[...]
    total_ref[:, i * n : (i + 1) * n] = base_ref[...] + product(got_ref[...], f_ref[i], width)
    rank = total_ref.shape[0] // 2
    share = rank // len(outs)
    for m, out in enumerate(outs):
        start = pl.multiple_of((me_ref[0] ^ m) * share, share)
        for q in range(2):
            out[q] = total_ref[pl.ds(q * rank + start, share), :]


def sum_kernel(*refs):
    *parts, out_ref = refs
    total = parts[0][...]
    for r in parts[1:]:
        total = total + r[...]
    out_ref[...] = total


def call(kernel, outs, *args, specs=None, scratch=(), name=None):
    return pl.pallas_call(
        kernel,
        out_shape=outs,
        in_specs=specs or [VMEM] * len(args),
        out_specs=jax.tree.map(lambda _: VMEM, outs),
        scratch_shapes=scratch,
        compiler_params=pltpu.CompilerParams(vmem_limit_bytes=16 * 2**20),
        name=name,
    )(*args)


def per_device(coefficients, factors):
    middle = (lax.axis_size("bis").bit_length() - 1) // 2
    rank, columns, blocks = coefficients.shape[2], coefficients.shape[3], factors.shape[2]
    width = columns // blocks
    step = columns // CHUNKS
    groups = lax.axis_size("src")
    f32 = jnp.float32
    raw = coefficients.reshape(2 * rank, columns)
    one = raw[:, step:]
    one, rest = lax.optimization_barrier((one, raw))
    states = [rest[:, :step], one]
    gots = [swapped(s, "bis", 2 ** (middle + 1)) for s in states]
    stacked = jax.ShapeDtypeStruct((CHUNKS, blocks // CHUNKS * rank, 4 * rank), jnp.bfloat16)
    halves = call(
        prepare_kernel, [stacked] * (2 * LEVELS), factors, name="prepare",
    )
    me = jnp.reshape(lax.axis_index("src"), (1,)).astype(jnp.int32)
    shape = jax.ShapeDtypeStruct((2 * rank, step), f32)
    piece = jax.ShapeDtypeStruct((2, rank // groups, columns), f32)
    order = tuple(reversed(range(CHUNKS)))
    for level in range(LEVELS):
        own, other = halves[2 * level : 2 * level + 2]
        for i in order:
            kw = dict(i=i, width=width)
            if level == LEVELS - 1 and i == order[0]:
                states[i] = call(
                    functools.partial(both_kernel, **kw), shape, states[i], gots[i], own, other,
                    name=f"level{level}_{i}",
                )
                if level < LEVELS - 1:
                    gots[i] = swapped(states[i], "bis", 2 ** (middle - level))
                continue
            if level:
                base = call(
                    functools.partial(own_kernel, **kw), shape, states[i], own, name=f"own{level}_{i}"
                )
            else:
                if i == order[0]:
                    bases = call(
                        functools.partial(owns_kernel, width=width), [shape] * CHUNKS, *states, own,
                        name="own0",
                    )
                base = bases[i]
            if (level, i) == (LEVELS - 1, order[-1]):
                pieces = call(
                    functools.partial(last_kernel, **kw), [piece] * groups,
                    me, states[order[0]], base, gots[i], other, specs=[SMEM] + [VMEM] * 4,
                    scratch=[pltpu.VMEM((2 * rank, columns), f32)], name="last",
                )
                continue
            states[i] = call(
                functools.partial(level_kernel, **kw), shape, base, gots[i], other,
                name=f"level{level}_{i}",
            )
            if level < LEVELS - 1:
                gots[i] = swapped(states[i], "bis", 2 ** (middle - level))
    parts = [pieces[0]] + [swapped(pieces[m], "src", m) for m in reversed(range(1, groups))]
    return call(sum_kernel, piece, *parts, name="total")


def solution(mesh):
    placed = (P("src", None, None, "bis"), P("src", None, "bis", None, None))
    return jax.shard_map(
        per_device, mesh=mesh, in_specs=placed, out_specs=P(None, "src", "bis"), check_vma=False
    )
```

```python
import functools
import jax
import jax.numpy as jnp
from jax import lax
from jax.experimental import pallas as pl
from jax.experimental.pallas import tpu as pltpu
from jax.sharding import PartitionSpec as P

LEVELS = 3
CHUNKS = 2
VMEM = pl.BlockSpec(memory_space=pltpu.MemorySpace.VMEM)
SMEM = pl.BlockSpec(memory_space=pltpu.MemorySpace.SMEM)
ANY = pl.BlockSpec(memory_space=pl.ANY)


def swapped(value, axis, mask):
    pairs = [(source, source ^ mask) for source in range(lax.axis_size(axis))]
    return lax.ppermute(value, axis, pairs)


def split(value):
    high = value.astype(jnp.bfloat16)
    low = (value - high.astype(jnp.float32)).astype(jnp.bfloat16)
    return high, low


def product(state, factor, width):
    rank, n = state.shape[0] // 2, state.shape[1]
    re, im = state[:rank], state[rank:]
    stack = jnp.concatenate(
        [jnp.concatenate([re, -im], axis=0), jnp.concatenate([im, re], axis=0)], axis=1
    )
    lane = lax.broadcasted_iota(jnp.int32, stack.shape, 1) % n
    zero = jnp.zeros_like(stack)
    stack = jnp.concatenate(
        [jnp.where(lane < n // 2, stack, zero), jnp.where(lane < n // 2, zero, stack)], axis=0
    )
    high, low = split(stack)
    rows = factor.shape[0] // 2
    dot = functools.partial(jnp.dot, preferred_element_type=jnp.float32)
    full = dot(factor[:rows], high) + dot(factor[:rows], low) + dot(factor[rows:], high)
    block = lax.broadcasted_iota(jnp.int32, (rank, 2 * n), 1) % (n // 2) // width
    out = full[:rank]
    for p in range(1, rows // rank):
        out = jnp.where(block == p, full[p * rank : (p + 1) * rank], out)
    return jnp.concatenate([out[:, :n], out[:, n:]], axis=0)


def prepare_kernel(f_hbm, *refs):
    outs, f_ref = refs, f_hbm.at[0]
    rank, depth = f_ref.shape[2:]
    half = depth // 2
    for level in range(LEVELS):
        chunks, rows, _ = outs[2 * level].shape
        rows = rows // 2
        per = rows // rank
        for c in range(chunks):
            for u in range(2):
                first = (2 * c + u) * per
                high, low = split(f_ref[level, first : first + per].reshape(rows, depth))
                side = slice(u * half, (u + 1) * half)
                for part in range(2):
                    out = outs[2 * level + part]
                    out[c, :rows, side] = high[:, part * half : (part + 1) * half]
                    out[c, rows:, side] = low[:, part * half : (part + 1) * half]


def own_kernel(own_ref, f_ref, out_ref, *, i, width):
    out_ref[...] = product(own_ref[...], f_ref[i], width)


def owns_kernel(*refs, width):
    f_ref = refs[CHUNKS]
    for i, out in enumerate(refs[CHUNKS + 1 :]):
        out[...] = product(refs[i][...], f_ref[i], width)


def level_kernel(base_ref, got_ref, f_ref, out_ref, *, i, width):
    out_ref[...] = base_ref[...] + product(got_ref[...], f_ref[i], width)


def last_kernel(me_ref, done_ref, base_ref, got_ref, f_ref, *refs, i, width):
    *outs, total_ref = refs
    n = got_ref.shape[1]
    other = 1 - i
    total_ref[:, other * n : (other + 1) * n] = done_ref[...]
    total_ref[:, i * n : (i + 1) * n] = base_ref[...] + product(got_ref[...], f_ref[i], width)
    rank = total_ref.shape[0] // 2
    share = rank // len(outs)
    for m, out in enumerate(outs):
        start = pl.multiple_of((me_ref[0] ^ m) * share, share)
        for q in range(2):
            out[q] = total_ref[pl.ds(q * rank + start, share), :]


def call(kernel, outs, *args, specs=None, scratch=(), name=None):
    return pl.pallas_call(
        kernel,
        out_shape=outs,
        in_specs=specs or [VMEM] * len(args),
        out_specs=jax.tree.map(lambda _: VMEM, outs),
        scratch_shapes=scratch,
        compiler_params=pltpu.CompilerParams(vmem_limit_bytes=16 * 2**20),
        name=name,
    )(*args)


def per_device(coefficients, factors):
    middle = (lax.axis_size("bis").bit_length() - 1) // 2
    rank, columns, blocks = coefficients.shape[2], coefficients.shape[3], factors.shape[2]
    width = columns // blocks
    step = columns // CHUNKS
    groups = lax.axis_size("src")
    f32 = jnp.float32
    raw = coefficients.reshape(2 * rank, columns)
    one = raw[:, step:]
    one, rest = lax.optimization_barrier((one, raw))
    states = [rest[:, :step], one]
    gots = [swapped(s, "bis", 2 ** (middle + 1)) for s in states]
    stacked = jax.ShapeDtypeStruct((CHUNKS, blocks // CHUNKS * rank, 4 * rank), jnp.bfloat16)
    halves = call(
        prepare_kernel, [stacked] * (2 * LEVELS), factors, name="prepare",
    )
    me = jnp.reshape(lax.axis_index("src"), (1,)).astype(jnp.int32)
    shape = jax.ShapeDtypeStruct((2 * rank, step), f32)
    piece = jax.ShapeDtypeStruct((2, rank // groups, columns), f32)
    order = tuple(reversed(range(CHUNKS)))
    for level in range(LEVELS):
        own, other = halves[2 * level : 2 * level + 2]
        for i in order:
            kw = dict(i=i, width=width)
            if level:
                base = call(
                    functools.partial(own_kernel, **kw), shape, states[i], own, name=f"own{level}_{i}"
                )
            else:
                if i == order[0]:
                    bases = call(
                        functools.partial(owns_kernel, width=width), [shape] * CHUNKS, *states, own,
                        name="own0",
                    )
                base = bases[i]
            if (level, i) == (LEVELS - 1, order[-1]):
                pieces = call(
                    functools.partial(last_kernel, **kw), [piece] * groups,
                    me, states[order[0]], base, gots[i], other, specs=[SMEM] + [VMEM] * 4,
                    scratch=[pltpu.VMEM((2 * rank, columns), f32)], name="last",
                )
                continue
            states[i] = call(
                functools.partial(level_kernel, **kw), shape, base, gots[i], other,
                name=f"level{level}_{i}",
            )
            if level < LEVELS - 1:
                gots[i] = swapped(states[i], "bis", 2 ** (middle - level))
    parts = [pieces[0]] + [swapped(pieces[m], "src", m) for m in reversed(range(1, groups))]
    total = parts[0]
    for p in parts[1:]:
        total = total + p
    return total


def solution(mesh):
    placed = (P("src", None, None, "bis"), P("src", None, "bis", None, None))
    return jax.shard_map(
        per_device, mesh=mesh, in_specs=placed, out_specs=P(None, "src", "bis"), check_vma=False
    )
```

```python
import functools
import jax
import jax.numpy as jnp
from jax import lax
from jax.experimental import pallas as pl
from jax.experimental.pallas import tpu as pltpu
from jax.sharding import PartitionSpec as P

LEVELS = 3
CHUNKS = 2
VMEM = pl.BlockSpec(memory_space=pltpu.MemorySpace.VMEM)
SMEM = pl.BlockSpec(memory_space=pltpu.MemorySpace.SMEM)
ANY = pl.BlockSpec(memory_space=pl.ANY)


def swapped(value, axis, mask):
    pairs = [(source, source ^ mask) for source in range(lax.axis_size(axis))]
    return lax.ppermute(value, axis, pairs)


def split(value):
    high = value.astype(jnp.bfloat16)
    low = (value - high.astype(jnp.float32)).astype(jnp.bfloat16)
    return high, low


def product(state, factor, width):
    rank, n = state.shape[0] // 2, state.shape[1]
    re, im = state[:rank], state[rank:]
    stack = jnp.concatenate(
        [jnp.concatenate([re, -im], axis=0), jnp.concatenate([im, re], axis=0)], axis=1
    )
    lane = lax.broadcasted_iota(jnp.int32, stack.shape, 1) % n
    zero = jnp.zeros_like(stack)
    stack = jnp.concatenate(
        [jnp.where(lane < n // 2, stack, zero), jnp.where(lane < n // 2, zero, stack)], axis=0
    )
    high, low = split(stack)
    rows = factor.shape[0] // 2
    dot = functools.partial(jnp.dot, preferred_element_type=jnp.float32)
    full = dot(factor[:rows], high) + dot(factor[rows:], high) + dot(factor[:rows], low)
    block = lax.broadcasted_iota(jnp.int32, (rank, 2 * n), 1) % (n // 2) // width
    out = full[:rank]
    for p in range(1, rows // rank):
        out = jnp.where(block == p, full[p * rank : (p + 1) * rank], out)
    return jnp.concatenate([out[:, :n], out[:, n:]], axis=0)


def prepare_kernel(f_hbm, *refs):
    outs, f_ref = refs, f_hbm.at[0]
    rank, depth = f_ref.shape[2:]
    half = depth // 2
    for level in range(LEVELS):
        chunks, rows, _ = outs[2 * level].shape
        rows = rows // 2
        per = rows // rank
        for c in range(chunks):
            for u in range(2):
                first = (2 * c + u) * per
                high, low = split(f_ref[level, first : first + per].reshape(rows, depth))
                side = slice(u * half, (u + 1) * half)
                for part in range(2):
                    out = outs[2 * level + part]
                    out[c, :rows, side] = high[:, part * half : (part + 1) * half]
                    out[c, rows:, side] = low[:, part * half : (part + 1) * half]


def own_kernel(own_ref, f_ref, out_ref, *, i, width):
    out_ref[...] = product(own_ref[...], f_ref[i], width)


def owns_kernel(*refs, width):
    f_ref = refs[CHUNKS]
    for i, out in enumerate(refs[CHUNKS + 1 :]):
        out[...] = product(refs[i][...], f_ref[i], width)


def level_kernel(base_ref, got_ref, f_ref, out_ref, *, i, width):
    out_ref[...] = base_ref[...] + product(got_ref[...], f_ref[i], width)


def last_kernel(me_ref, done_ref, base_ref, got_ref, f_ref, *refs, i, width):
    *outs, total_ref = refs
    n = got_ref.shape[1]
    other = 1 - i
    total_ref[:, other * n : (other + 1) * n] = done_ref[...]
    total_ref[:, i * n : (i + 1) * n] = base_ref[...] + product(got_ref[...], f_ref[i], width)
    rank = total_ref.shape[0] // 2
    share = rank // len(outs)
    for m, out in enumerate(outs):
        start = pl.multiple_of((me_ref[0] ^ m) * share, share)
        for q in range(2):
            out[q] = total_ref[pl.ds(q * rank + start, share), :]


def call(kernel, outs, *args, specs=None, scratch=(), name=None):
    return pl.pallas_call(
        kernel,
        out_shape=outs,
        in_specs=specs or [VMEM] * len(args),
        out_specs=jax.tree.map(lambda _: VMEM, outs),
        scratch_shapes=scratch,
        compiler_params=pltpu.CompilerParams(vmem_limit_bytes=16 * 2**20),
        name=name,
    )(*args)


def per_device(coefficients, factors):
    middle = (lax.axis_size("bis").bit_length() - 1) // 2
    rank, columns, blocks = coefficients.shape[2], coefficients.shape[3], factors.shape[2]
    width = columns // blocks
    step = columns // CHUNKS
    groups = lax.axis_size("src")
    f32 = jnp.float32
    raw = coefficients.reshape(2 * rank, columns)
    one = raw[:, step:]
    one, rest = lax.optimization_barrier((one, raw))
    states = [rest[:, :step], one]
    gots = [swapped(s, "bis", 2 ** (middle + 1)) for s in states]
    stacked = jax.ShapeDtypeStruct((CHUNKS, blocks // CHUNKS * rank, 4 * rank), jnp.bfloat16)
    halves = call(
        prepare_kernel, [stacked] * (2 * LEVELS), factors, name="prepare",
    )
    me = jnp.reshape(lax.axis_index("src"), (1,)).astype(jnp.int32)
    shape = jax.ShapeDtypeStruct((2 * rank, step), f32)
    piece = jax.ShapeDtypeStruct((2, rank // groups, columns), f32)
    order = tuple(reversed(range(CHUNKS)))
    for level in range(LEVELS):
        own, other = halves[2 * level : 2 * level + 2]
        for i in order:
            kw = dict(i=i, width=width)
            if level:
                base = call(
                    functools.partial(own_kernel, **kw), shape, states[i], own, name=f"own{level}_{i}"
                )
            else:
                if i == order[0]:
                    bases = call(
                        functools.partial(owns_kernel, width=width), [shape] * CHUNKS, *states, own,
                        name="own0",
                    )
                base = bases[i]
            if (level, i) == (LEVELS - 1, order[-1]):
                pieces = call(
                    functools.partial(last_kernel, **kw), [piece] * groups,
                    me, states[order[0]], base, gots[i], other, specs=[SMEM] + [VMEM] * 4,
                    scratch=[pltpu.VMEM((2 * rank, columns), f32)], name="last",
                )
                continue
            states[i] = call(
                functools.partial(level_kernel, **kw), shape, base, gots[i], other,
                name=f"level{level}_{i}",
            )
            if level < LEVELS - 1:
                gots[i] = swapped(states[i], "bis", 2 ** (middle - level))
    parts = [pieces[0]] + [swapped(pieces[m], "src", m) for m in reversed(range(1, groups))]
    total = parts[0]
    for p in parts[1:]:
        total = total + p
    return total


def solution(mesh):
    placed = (P("src", None, None, "bis"), P("src", None, "bis", None, None))
    return jax.shard_map(
        per_device, mesh=mesh, in_specs=placed, out_specs=P(None, "src", "bis"), check_vma=False
    )
```

```python
import functools
import jax
import jax.numpy as jnp
from jax import lax
from jax.experimental import pallas as pl
from jax.experimental.pallas import tpu as pltpu
from jax.sharding import PartitionSpec as P

LEVELS = 3
CHUNKS = 2
VMEM = pl.BlockSpec(memory_space=pltpu.MemorySpace.VMEM)
SMEM = pl.BlockSpec(memory_space=pltpu.MemorySpace.SMEM)
ANY = pl.BlockSpec(memory_space=pl.ANY)


def swapped(value, axis, mask):
    pairs = [(source, source ^ mask) for source in range(lax.axis_size(axis))]
    return lax.ppermute(value, axis, pairs)


def split(value):
    high = value.astype(jnp.bfloat16)
    low = (value - high.astype(jnp.float32)).astype(jnp.bfloat16)
    return high, low


def product(state, factor, width):
    rank, n = state.shape[0] // 2, state.shape[1]
    re, im = state[:rank], state[rank:]
    stack = jnp.concatenate(
        [jnp.concatenate([re, -im], axis=0), jnp.concatenate([im, re], axis=0)], axis=1
    )
    lane = lax.broadcasted_iota(jnp.int32, stack.shape, 1) % n
    zero = jnp.zeros_like(stack)
    stack = jnp.concatenate(
        [jnp.where(lane < n // 2, stack, zero), jnp.where(lane < n // 2, zero, stack)], axis=0
    )
    high, low = split(stack)
    rows = factor.shape[0] // 2
    dot = functools.partial(jnp.dot, preferred_element_type=jnp.float32)
    full = dot(factor[:rows], high) + dot(factor[rows:], high) + dot(factor[:rows], low)
    block = lax.broadcasted_iota(jnp.int32, (rank, 2 * n), 1) % (n // 2) // width
    out = full[:rank]
    for p in range(1, rows // rank):
        out = jnp.where(block == p, full[p * rank : (p + 1) * rank], out)
    return jnp.concatenate([out[:, :n], out[:, n:]], axis=0)


def prepare_kernel(f_hbm, *refs):
    outs, f_ref = refs, f_hbm.at[0]
    rank, depth = f_ref.shape[2:]
    half = depth // 2
    for level in range(LEVELS):
        chunks, rows, _ = outs[2 * level].shape
        rows = rows // 2
        per = rows // rank
        for c in range(chunks):
            for u in range(2):
                first = (2 * c + u) * per
                high, low = split(f_ref[level, first : first + per].reshape(rows, depth))
                side = slice(u * half, (u + 1) * half)
                for part in range(2):
                    out = outs[2 * level + part]
                    out[c, :rows, side] = high[:, part * half : (part + 1) * half]
                    out[c, rows:, side] = low[:, part * half : (part + 1) * half]


def owns_kernel(*refs, width):
    f_ref = refs[CHUNKS]
    for i, out in enumerate(refs[CHUNKS + 1 :]):
        out[...] = product(refs[i][...], f_ref[i], width)


def level_kernel(base_ref, got_ref, f_ref, out_ref, *, i, width):
    out_ref[...] = base_ref[...] + product(got_ref[...], f_ref[i], width)


def last_kernel(me_ref, done_ref, base_ref, got_ref, f_ref, *refs, i, width):
    *outs, total_ref = refs
    n = got_ref.shape[1]
    other = 1 - i
    total_ref[:, other * n : (other + 1) * n] = done_ref[...]
    total_ref[:, i * n : (i + 1) * n] = base_ref[...] + product(got_ref[...], f_ref[i], width)
    rank = total_ref.shape[0] // 2
    share = rank // len(outs)
    for m, out in enumerate(outs):
        start = pl.multiple_of((me_ref[0] ^ m) * share, share)
        for q in range(2):
            out[q] = total_ref[pl.ds(q * rank + start, share), :]


def call(kernel, outs, *args, specs=None, scratch=(), name=None):
    return pl.pallas_call(
        kernel,
        out_shape=outs,
        in_specs=specs or [VMEM] * len(args),
        out_specs=jax.tree.map(lambda _: VMEM, outs),
        scratch_shapes=scratch,
        compiler_params=pltpu.CompilerParams(vmem_limit_bytes=16 * 2**20),
        name=name,
    )(*args)


def per_device(coefficients, factors):
    middle = (lax.axis_size("bis").bit_length() - 1) // 2
    rank, columns, blocks = coefficients.shape[2], coefficients.shape[3], factors.shape[2]
    width = columns // blocks
    step = columns // CHUNKS
    groups = lax.axis_size("src")
    f32 = jnp.float32
    raw = coefficients.reshape(2 * rank, columns)
    one = raw[:, step:]
    one, rest = lax.optimization_barrier((one, raw))
    states = [rest[:, :step], one]
    gots = [swapped(s, "bis", 2 ** (middle + 1)) for s in states]
    stacked = jax.ShapeDtypeStruct((CHUNKS, blocks // CHUNKS * rank, 4 * rank), jnp.bfloat16)
    halves = call(
        prepare_kernel, [stacked] * (2 * LEVELS), factors, name="prepare",
    )
    me = jnp.reshape(lax.axis_index("src"), (1,)).astype(jnp.int32)
    shape = jax.ShapeDtypeStruct((2 * rank, step), f32)
    piece = jax.ShapeDtypeStruct((2, rank // groups, columns), f32)
    order = tuple(reversed(range(CHUNKS)))
    for level in range(LEVELS):
        own, other = halves[2 * level : 2 * level + 2]
        for i in order:
            kw = dict(i=i, width=width)
            if i == order[0]:
                bases = call(
                    functools.partial(owns_kernel, width=width), [shape] * CHUNKS, *states, own,
                    name=f"own{level}",
                )
            base = bases[i]
            if (level, i) == (LEVELS - 1, order[-1]):
                pieces = call(
                    functools.partial(last_kernel, **kw), [piece] * groups,
                    me, states[order[0]], base, gots[i], other, specs=[SMEM] + [VMEM] * 4,
                    scratch=[pltpu.VMEM((2 * rank, columns), f32)], name="last",
                )
                continue
            states[i] = call(
                functools.partial(level_kernel, **kw), shape, base, gots[i], other,
                name=f"level{level}_{i}",
            )
            if level < LEVELS - 1:
                gots[i] = swapped(states[i], "bis", 2 ** (middle - level))
    parts = [pieces[0]] + [swapped(pieces[m], "src", m) for m in reversed(range(1, groups))]
    total = parts[0]
    for p in parts[1:]:
        total = total + p
    return total


def solution(mesh):
    placed = (P("src", None, None, "bis"), P("src", None, "bis", None, None))
    return jax.shard_map(
        per_device, mesh=mesh, in_specs=placed, out_specs=P(None, "src", "bis"), check_vma=False
    )
```
